32 devices in a mesh: groups: 2 (over y), unit: 4 (over z), week: 2 (over x), region: 2 (over core).
Axes of the slice: x: 2, y: 2, z: 4, core: 2. Of those that a mesh axis runs over, the one named last changes fastest.
Arguments:
- flow_start: float32 [8, 4, 64, 8192], P(('groups', 'unit'), ('week', 'region')), parts along dimension 0, may hold values from 0 to 2
- node_start: float32 [8, 4, 64, 512], P(('groups', 'unit'), ('week', 'region')), parts along dimension 0, may hold values from -6 to 6
- seat_start: float32 [8, 64, 4096], P(('groups', 'week', 'region')), parts along dimension 0, may hold values from 0 to 4
- arc_cost: float32 [8, 4, 8192], P(('groups', 'unit'), ('week', 'region')), parts along dimension 0, may hold values from 0.05 to 25
- demand: float32 [8, 64, 4096], P(('groups', 'week', 'region')), parts along dimension 0, may hold values from 0.02 to 50
- seat_counts: float32 [8], P(('groups', 'unit')), parts along dimension 0, may hold values from 0.25 to 4
- tail_node: int32 [8, 4, 8192], P(('groups', 'unit'), ('week', 'region')), parts along dimension 0, may hold values from 0 to 511, as said below
- head_node: int32 [8, 4, 8192], P(('groups', 'unit'), ('week', 'region')), parts along dimension 0, may hold values from 0 to 511, as said below
- cover_row: int32 [8, 4, 4096], P(('groups', 'unit'), ('week', 'region')), parts along dimension 0, may hold values from 0 to 4095, as said below
Outputs:
- flows: float32 [8, 4, 64, 8192], P(('groups', 'unit'), ('week', 'region')), parts along dimension 0
- node_prices: float32 [8, 4, 64, 512], P(('groups', 'unit'), ('week', 'region')), parts along dimension 0
- seat_prices: float32 [8, 64, 4096], P(('groups', 'week', 'region')), parts along dimension 0
The draws below stay inside these ranges and needn't reach their ends.
There are 2 independent parts, one for each index of `groups`. The reference program is written for one: setup_inputs(seed, part) draws one part's arguments, and reference() takes and returns one part's arrays. A program takes and returns all parts, laid end to end along the dimension named above; each array names one. Nothing has to cross between parts.
Inputs may be any that keep to these rules, and one draw needn't show every extreme that they name: `tail_node`: in each aligned block of 128 arcs of one unit type and slice, all tail nodes lie in one aligned block of 128 nodes. `head_node`: in each aligned block of 128 arcs of one unit type and slice, all head nodes lie in one aligned block of 128 nodes of the slice that holds them. `cover_row`: in each aligned block of 128 trip arcs of one unit type and slice, all rows lie in one aligned block of 128 rows.
All inputs are finite; a program needn't handle non-finite values.
Results may differ from the reference program's by a relative error of at most 0.0001.
Values sent between devices are 32-bit elements; how exact they have to be, the bound alone decides.
A program may use at most 64 MiB of HBM per device.

```python
import math
import jax
import jax.numpy as jnp
from jax import lax

SCEN = 64
ARC_DEV = 8192
NODE_DEV = 512
TRIP_DEV = 4096
ITERS = 2
UNITS = 4
SLICES = 4
WRAP_ARCS = 1024
CROSS_ARCS = 1024
TRIP_ARCS = 4096


def blocked_index(key, item_count, extent):
    block_count = item_count // 128
    chosen = jax.random.randint(jax.random.fold_in(key, 1), (UNITS * SLICES, block_count, 1), 0, extent // 128)
    offsets = jax.random.randint(jax.random.fold_in(key, 2), (UNITS * SLICES, block_count, 128), 0, 128)
    return (chosen * 128 + offsets).reshape(UNITS, SLICES, item_count).astype(jnp.int32)


def draw_tail_node(key, part):
    return blocked_index(jax.random.fold_in(key, 101), ARC_DEV, NODE_DEV)


def draw_head_node(key, part):
    return blocked_index(jax.random.fold_in(key, 202), ARC_DEV, NODE_DEV)


def draw_cover_row(key, part):
    return blocked_index(jax.random.fold_in(key, 303), TRIP_ARCS, TRIP_DEV)


def position_ramp(total):
    return jnp.arange(total, dtype=jnp.float32) / max(total - 1, 1)


def draw_arc_cost(key, part):
    array_shape = (UNITS, SLICES, ARC_DEV)
    base_cost = jnp.exp(jax.random.uniform(key, array_shape, jnp.float32, math.log(0.1), 0.0))
    growth = 3.0
    position_sum = position_ramp(UNITS)[:, None, None] + position_ramp(SLICES)[None, :, None]
    return base_cost * jnp.power(growth, position_sum)


def draw_demand(key, part):
    cell_key = jax.random.fold_in(key, 11)
    row_key = jax.random.fold_in(key, 12)
    column_key = jax.random.fold_in(key, 13)
    array_shape = (SLICES, SCEN, TRIP_DEV)
    row_scale = jnp.exp(jax.random.uniform(row_key, (SLICES, 1, TRIP_DEV), jnp.float32, 0.0, math.log(10.0))) / math.sqrt(10.0)
    column_scale = jnp.exp(jax.random.uniform(column_key, (1, SCEN, 1), jnp.float32, 0.0, math.log(10.0))) / math.sqrt(10.0)
    cell_value = jnp.exp(jax.random.uniform(cell_key, array_shape, jnp.float32, math.log(0.25), 0.0))
    growth = 3.0
    return cell_value * row_scale * column_scale * jnp.power(growth, position_ramp(SLICES))[:, None, None]


def block_levels(rng, shape, cuts, least, high):
    gain = 1.0
    for axis_at, blocks in cuts:
        draws = jax.random.uniform(jax.random.fold_in(jax.random.fold_in(rng, 6), axis_at), (blocks,), jnp.float32, least / len(cuts), high / len(cuts))
        gain = gain * jnp.repeat(jnp.exp(draws), shape[axis_at] // blocks).reshape((-1,) + (1,) * (len(shape) - 1 - axis_at))
    return gain


def normal_values(stream_key, dims, spread, reach, split=(), kind=jnp.bfloat16):
    array = jax.random.normal(stream_key, dims, jnp.float32) * spread
    if len(split) > 0:
        array = block_levels(stream_key, dims, split, -0.22, 0.18) * array
    return jnp.clip(array, min=-reach, max=reach).astype(kind)


def setup_inputs(seed: int = 0, part: int = 0) -> dict:
    streams_of = jax.random.split(jax.random.key(seed), 10)
    own_keys = jax.random.split(jax.random.fold_in(streams_of[9], part), 10)
    flow_start = jnp.clip(2.0 * jax.random.uniform(own_keys[0], (UNITS, SLICES, SCEN, ARC_DEV), jnp.float32) ** block_levels(own_keys[0], (UNITS, SLICES, SCEN, ARC_DEV), ((0, 4), (1, 4)), -0.2, 0.2), 0.0, 2.0)
    node_start = normal_values(own_keys[1], (UNITS, SLICES, SCEN, NODE_DEV), 1.0, 6.0, ((0, 4), (1, 4)), jnp.float32)
    seat_start = jnp.clip(4.0 * jax.random.uniform(own_keys[2], (SLICES, SCEN, TRIP_DEV), jnp.float32) ** block_levels(own_keys[2], (SLICES, SCEN, TRIP_DEV), ((0, 4),), -0.2, 0.2), 0.0, 4.0)
    arc_cost = draw_arc_cost(jax.random.fold_in(jax.random.fold_in(streams_of[9], part), 71), part)
    demand = draw_demand(jax.random.fold_in(jax.random.fold_in(streams_of[9], part), 71), part)
    seat_counts = jnp.clip(jnp.exp(math.log(4.0) - 2.7725887 * jax.random.uniform(own_keys[5], (UNITS,), jnp.float32) ** block_levels(own_keys[5], (UNITS,), ((0, 4),), -0.2, 0.2)), 0.25, 4.0)
    tail_node = draw_tail_node(jax.random.fold_in(jax.random.fold_in(streams_of[9], part), 71), part)
    head_node = draw_head_node(jax.random.fold_in(jax.random.fold_in(streams_of[9], part), 71), part)
    cover_row = draw_cover_row(jax.random.fold_in(jax.random.fold_in(streams_of[9], part), 71), part)
    return dict(flow_start=flow_start, node_start=node_start, seat_start=seat_start, arc_cost=arc_cost, demand=demand, seat_counts=seat_counts, tail_node=tail_node, head_node=head_node, cover_row=cover_row)


EPS = 1e-06
STEP = 0.5

def add_rows(values, index, extent):

    def one_slice(part_values, part_index):
        return jax.ops.segment_sum(part_values.T, part_index, num_segments=extent).T
    return jax.vmap(one_slice)(values, index)

def pick_rows(field, index):
    return jnp.take_along_axis(field, index[:, None, :], axis=2)

def reference(flow_start, node_start, seat_start, arc_cost, demand, seat_counts, tail_node, head_node, cover_row):
    cost_total = jnp.sum(arc_cost * arc_cost)
    demand_total = lax.optimization_barrier(jnp.sum(demand * demand, axis=(0, 2)))
    weight_ratio = jnp.sqrt((cost_total / (UNITS * SLICES * ARC_DEV) + EPS) / (demand_total / (SLICES * TRIP_DEV) + EPS))
    primal_step = (STEP / weight_ratio)[:, None]
    dual_step = (STEP * weight_ratio)[:, None]
    position = jnp.arange(ARC_DEV, dtype=jnp.int32)
    arc_group = (position >= ARC_DEV - WRAP_ARCS - CROSS_ARCS).astype(jnp.int32) + (position >= ARC_DEV - CROSS_ARCS).astype(jnp.int32)
    head_wide = (head_node + arc_group[None, None, :] * NODE_DEV).astype(jnp.int32)
    week_count = SLICES // 2
    flow_now, prices, covers = (flow_start, node_start, seat_start)
    for iteration in range(ITERS):

        def unit_step(seat_total, unit_data):
            flow_u, price_u, cost_u, seat_u, tail_u, head_u, row_u = unit_data
            price_grid = price_u.reshape(week_count, 2, SCEN, NODE_DEV)
            price_next = jnp.roll(price_grid, -1, axis=0).reshape(SLICES, SCEN, NODE_DEV)
            price_other = jnp.flip(price_grid, axis=1).reshape(SLICES, SCEN, NODE_DEV)
            extended = jnp.concatenate([price_u, price_next, price_other], axis=2)
            seat_scale = seat_u / UNITS
            cover_terms = seat_scale * pick_rows(covers, row_u)
            cover_terms = jnp.concatenate([cover_terms, jnp.zeros((SLICES, SCEN, ARC_DEV - TRIP_ARCS), jnp.float32)], axis=2)
            gradient = cost_u[:, None, :] - cover_terms - (pick_rows(extended, head_u) - pick_rows(price_u, tail_u))
            updated = jnp.maximum(flow_u - primal_step * gradient, 0.0)
            extrapolated = 2.0 * updated - flow_u
            inflow = add_rows(extrapolated, head_u, 3 * NODE_DEV)
            outflow = add_rows(extrapolated, tail_u, NODE_DEV)
            sent_next = inflow[:, :, NODE_DEV:2 * NODE_DEV].reshape(week_count, 2, SCEN, NODE_DEV)
            sent_other = inflow[:, :, 2 * NODE_DEV:].reshape(week_count, 2, SCEN, NODE_DEV)
            arrived_next = jnp.roll(sent_next, 1, axis=0).reshape(SLICES, SCEN, NODE_DEV)
            arrived_other = jnp.flip(sent_other, axis=1).reshape(SLICES, SCEN, NODE_DEV)
            balance = inflow[:, :, :NODE_DEV] + arrived_next + arrived_other - outflow
            seat_part = add_rows(seat_scale * extrapolated[:, :, :TRIP_ARCS], row_u, TRIP_DEV)
            return (seat_total + seat_part, (updated, price_u - dual_step * balance))
        seat_total, (flow_now, prices) = lax.scan(unit_step, jnp.zeros((SLICES, SCEN, TRIP_DEV), jnp.float32), (flow_now, prices, arc_cost, seat_counts, tail_node, head_wide, cover_row))
        covers = jnp.maximum(covers + dual_step * (demand - seat_total), 0.0)
    return (flow_now, prices, covers)
```

```python
import functools

import jax
import jax.numpy as jnp
from jax import lax
from jax.experimental import pallas as pl
from jax.experimental.pallas import tpu as pltpu
from jax.sharding import PartitionSpec as P

ITERS = 2
WRAP_ARCS = 1024
CROSS_ARCS = 1024
EPS = 1e-06
STEP = 0.5
CHUNKS = 4
UNROLL = 8
MESH = pl.DeviceIdType.MESH
F32 = jnp.float32
BF16 = jnp.bfloat16


def split_rows(value):
    high = value.astype(BF16)
    low = (value - high.astype(F32)).astype(BF16)
    return jnp.concatenate([high, low], axis=0)


def pick(block, index):
    return jnp.take_along_axis(block, index, axis=1, mode="promise_in_bounds")


def kernel(
    units, weeks, chunks,
    flow_ref, node_ref, seat_ref, cost_ref, demand_ref, count_ref, tail_ref, head_ref, cover_ref,
    meta_ref,
    flow_out, node_out, seat_out,
    hot_ends, hot_cover, covers, price_local, chain, own_price, recv_price, own_balance, send_in,
    recv_in, part, send_right, send_left, recv_right, recv_left, stat_mine, stat_slices, cost_mine,
    cost_units, primal, dual,
    stat_send, stat_recv, unit_send, unit_recv, price_send, price_recv, in_send, in_recv,
    right_send, right_recv, left_send, left_recv,
):
    me = lax.axis_index("unit")
    week = lax.axis_index("week")
    region = lax.axis_index("region")
    scen, arcs = flow_ref.shape
    nodes = node_ref.shape[1]
    trips = seat_ref.shape[1]
    rows = scen // chunks
    node_blocks = nodes // 128
    trip_blocks = trips // 128
    arc_blocks = arcs // 128
    cover_blocks = cover_ref.shape[0]
    slices = 2 * weeks
    mine = week * 2 + region
    ahead = lax.rem(week + 1, weeks)
    behind = lax.rem(week + weeks - 1, weeks)
    stride = max(chunks, units - 1)
    scale = count_ref[0] / units

    barrier = pltpu.get_barrier_semaphore()
    for step in range(1, units):
        other = lax.rem(me + step, units)
        pl.semaphore_signal(barrier, inc=1, device_id={"unit": other}, device_id_type=MESH)
    for step in range(1, slices):
        other = lax.rem(mine + step, slices)
        pl.semaphore_signal(
            barrier, inc=1, device_id={"week": other // 2, "region": other % 2},
            device_id_type=MESH,
        )

    demand_squares = jnp.zeros((scen, 128), F32)
    for block in range(trip_blocks):
        piece = demand_ref[:, block * 128 : block * 128 + 128]
        demand_squares += piece * piece
    cost_squares = jnp.zeros((8, 128), F32)
    for block in range(arc_blocks // 8):
        piece = cost_ref[block * 8 : block * 8 + 8, :]
        cost_squares += piece * piece
    stat_mine[0:scen, :] = demand_squares
    stat_mine[scen : scen + 8, :] = cost_squares
    for c in range(chunks):
        for block in range(node_blocks):
            own_price[c, block] = node_ref[
                c * rows : c * rows + rows, block * 128 : block * 128 + 128
            ]
    pl.semaphore_wait(barrier, units - 1 + slices - 1)

    def stat_copy(other, slot):
        return pltpu.make_async_remote_copy(
            src_ref=stat_mine, dst_ref=stat_slices.at[slot], send_sem=stat_send.at[other],
            recv_sem=stat_recv.at[slot],
            device_id={"week": other // 2, "region": other % 2}, device_id_type=MESH,
        )

    def unit_copy(other, slot):
        return pltpu.make_async_remote_copy(
            src_ref=cost_mine, dst_ref=cost_units.at[slot], send_sem=unit_send.at[other],
            recv_sem=unit_recv.at[slot], device_id={"unit": other}, device_id_type=MESH,
        )

    def price_copy(side, item):
        target = {"week": behind} if side == 0 else {"region": 1 - region}
        return pltpu.make_async_remote_copy(
            src_ref=own_price.at[item], dst_ref=recv_price.at[side, item],
            send_sem=price_send.at[side, item], recv_sem=price_recv.at[side, item],
            device_id=target, device_id_type=MESH,
        )

    def in_copy(side, item):
        target = {"week": ahead} if side == 0 else {"region": 1 - region}
        return pltpu.make_async_remote_copy(
            src_ref=send_in.at[side, item], dst_ref=recv_in.at[side, item],
            send_sem=in_send.at[side, item], recv_sem=in_recv.at[side, item],
            device_id=target, device_id_type=MESH,
        )

    def right_copy(item):
        return pltpu.make_async_remote_copy(
            src_ref=send_right.at[item], dst_ref=recv_right.at[item],
            send_sem=right_send.at[item], recv_sem=right_recv.at[item],
            device_id={"unit": lax.rem(me + 1, units)}, device_id_type=MESH,
        )

    def left_copy(item):
        return pltpu.make_async_remote_copy(
            src_ref=send_left.at[item], dst_ref=recv_left.at[item],
            send_sem=left_send.at[item], recv_sem=left_recv.at[item],
            device_id={"unit": lax.rem(me + units - 1, units)}, device_id_type=MESH,
        )

    for step in range(1, slices):
        stat_copy(lax.rem(mine + step, slices), mine).start()
    for c in range(chunks):
        price_copy(0, c).start()
        price_copy(1, c).start()

    sub = lax.broadcasted_iota(jnp.int32, (128, 128), 0)

    def hot(row):
        return jnp.where(jnp.broadcast_to(row, (128, 128)) == sub, 1.0, 0.0).astype(BF16)

    @pl.loop(0, arc_blocks // 8)
    def _(group):
        at = pl.ds(pl.multiple_of(group * 8, 8), 8)
        heads = head_ref[at, :] & 127
        tails = tail_ref[at, :] & 127
        for k in range(8):
            hot_ends[group * 8 + k, 0:128, :] = hot(heads[k : k + 1, :])
            hot_ends[group * 8 + k, 128:256, :] = hot(tails[k : k + 1, :])

    @pl.loop(0, cover_blocks // 8)
    def _(group):
        at = pl.ds(pl.multiple_of(group * 8, 8), 8)
        targets = cover_ref[at, :] & 127
        for k in range(8):
            hot_cover[group * 8 + k] = hot(targets[k : k + 1, :])

    for c in range(chunks):
        for block in range(trip_blocks):
            covers[c * trip_blocks + block] = seat_ref[
                c * rows : c * rows + rows, block * 128 : block * 128 + 128
            ]
    flow_out[...] = flow_ref[...]
    chain[0] = jnp.zeros((rows, 128), F32)

    @pl.when(me == 0)
    def _():
        recv_right[...] = jnp.zeros_like(recv_right)

    @pl.when(me == units - 1)
    def _():
        recv_left[...] = jnp.zeros_like(recv_left)

    for step in range(1, slices):
        stat_copy(mine, lax.rem(mine + step, slices)).wait_recv()
    stat_total = stat_mine[...]
    for step in range(1, slices):
        stat_total += stat_slices[lax.rem(mine + step, slices)]
    cost_mine[...] = stat_total[scen : scen + 8, :]
    for step in range(1, units):
        unit_copy(lax.rem(me + step, units), me).start()
    for step in range(1, units):
        unit_copy(me, lax.rem(me + step, units)).wait_recv()
    cost_total = cost_mine[...]
    for step in range(1, units):
        cost_total += cost_units[lax.rem(me + step, units)]
    cost_sum = jnp.sum(jnp.sum(cost_total, axis=0, keepdims=True), axis=1, keepdims=True)
    demand_sum = jnp.sum(stat_total[0:scen, :], axis=1, keepdims=True)
    ratio = jnp.sqrt(
        (cost_sum / (arcs * units * slices) + EPS) / (demand_sum / (trips * slices) + EPS)
    )
    primal[...] = jnp.broadcast_to(STEP / ratio, (scen, 128))
    dual[...] = jnp.broadcast_to(STEP * ratio, (scen, 128))

    head_at, tail_at = 0, arc_blocks
    cover_at = 2 * arc_blocks
    prev_at = cover_at + cover_blocks
    last_at = prev_at + cover_blocks
    cross = arc_blocks - CROSS_ARCS // 128
    wrap = cross - WRAP_ARCS // 128

    def compute(item, c):
        there = pl.ds(pl.multiple_of(c * rows, 8), rows)
        price_copy(0, item).wait_recv()
        price_copy(1, item).wait_recv()
        price_local[0:node_blocks] = own_price[item]
        price_local[node_blocks : 2 * node_blocks] = recv_price[0, item]
        price_local[2 * node_blocks : 3 * node_blocks] = recv_price[1, item]
        step_size = primal[there, :]

        def section(first, end, side, with_cover, start):
            def body(group, carry):
                own, away = list(carry[0]), list(carry[1])
                base = first + group * UNROLL
                at = pl.ds(pl.multiple_of(base, 8), UNROLL)
                heads = head_ref[at, :] & 127
                tails = tail_ref[at, :] & 127
                costs = cost_ref[at, :]
                if with_cover:
                    targets = cover_ref[at, :] & 127
                for k in range(UNROLL):
                    b = base + k
                    head_block = meta_ref[head_at + b]
                    tail_block = meta_ref[tail_at + b]
                    head_value = pick(
                        price_local[side * node_blocks + head_block],
                        jnp.broadcast_to(heads[k : k + 1, :], (rows, 128)),
                    )
                    tail_value = pick(
                        price_local[tail_block],
                        jnp.broadcast_to(tails[k : k + 1, :], (rows, 128)),
                    )
                    gradient = jnp.broadcast_to(costs[k : k + 1, :], (rows, 128))
                    if with_cover:
                        seat = pick(
                            covers[c * trip_blocks + meta_ref[cover_at + b]],
                            jnp.broadcast_to(targets[k : k + 1, :], (rows, 128)),
                        )
                        gradient = gradient - scale * seat
                    gradient = gradient - (head_value - tail_value)
                    column = pl.ds(pl.multiple_of(b * 128, 128), 128)
                    now = flow_out[there, column]
                    updated = jnp.maximum(now - step_size * gradient, 0.0)
                    flow_out[there, column] = updated
                    halves = split_rows(2.0 * updated - now)
                    ends = lax.dot_general(
                        halves, hot_ends[b], (((1,), (1,)), ((), ())),
                        preferred_element_type=F32,
                    )
                    ends = ends[0:rows] + ends[rows : 2 * rows]
                    into, outof = ends[:, 0:128], ends[:, 128:256]
                    for m in range(node_blocks):
                        landed = jnp.where(head_block == m, into, 0.0)
                        left = jnp.where(tail_block == m, outof, 0.0)
                        if side == 0:
                            own[m] = own[m] + (landed - left)
                        else:
                            own[m] = own[m] - left
                            away[m] = away[m] + landed
                    if with_cover:
                        filled = lax.dot_general(
                            halves, hot_cover[b], (((1,), (1,)), ((), ())),
                            preferred_element_type=F32,
                        )
                        filled = filled[0:rows] + filled[rows : 2 * rows]
                        chain[b + 1] = scale * filled + chain[meta_ref[prev_at + b]]
                return tuple(own), tuple(away)

            return lax.fori_loop(0, (end - first) // UNROLL, body, start)

        zeros = tuple(jnp.zeros((rows, 128), F32) for _ in range(node_blocks))
        own, _ = section(0, cover_blocks, 0, True, (zeros, ()))
        own, _ = section(cover_blocks, wrap, 0, False, (own, ()))
        own, away_next = section(wrap, cross, 1, False, (own, zeros))
        own, away_other = section(cross, arc_blocks, 2, False, (own, zeros))
        for m in range(node_blocks):
            own_balance[item, m] = own[m]
            send_in[0, item, m] = away_next[m]
            send_in[1, item, m] = away_other[m]
        in_copy(0, item).start()
        in_copy(1, item).start()
        for m in range(trip_blocks):
            part[item, m] = chain[meta_ref[last_at + m]]

    def settle_nodes(item, c, it):
        there = pl.ds(pl.multiple_of(c * rows, 8), rows)
        in_copy(0, item).wait_recv()
        in_copy(1, item).wait_recv()
        step_size = dual[there, :]

        def priced(m):
            balance = own_balance[item, m] + recv_in[0, item, m] + recv_in[1, item, m]
            return own_price[item, m] - step_size * balance

        @pl.when(it < ITERS - 1)
        def _():
            for m in range(node_blocks):
                own_price[item + chunks, m] = priced(m)
            price_copy(0, item + chunks).start()
            price_copy(1, item + chunks).start()

        @pl.when(it == ITERS - 1)
        def _():
            for m in range(node_blocks):
                node_out[there, m * 128 : m * 128 + 128] = priced(m)

    def settle_seats(item, c, it):
        there = pl.ds(pl.multiple_of(c * rows, 8), rows)
        step_size = dual[there, :]

        def covered(m):
            total = recv_right[item, m] + part[item, m] + recv_left[item, m]
            wanted = demand_ref[there, m * 128 : m * 128 + 128]
            return jnp.maximum(
                covers[c * trip_blocks + m] + step_size * (wanted - total), 0.0
            )

        @pl.when(it < ITERS - 1)
        def _():
            for m in range(trip_blocks):
                covers[c * trip_blocks + m] = covered(m)

        @pl.when(it == ITERS - 1)
        def _():
            for m in range(trip_blocks):
                seat_out[there, m * 128 : m * 128 + 128] = covered(m)

    def at_slot(slot, action):
        it = slot // stride
        c = slot % stride

        @pl.when((slot >= 0) & (c < chunks) & (it < ITERS))
        def _():
            action(it * chunks + c, c, it)

    def forward_right(item, c, it):
        @pl.when(me > 0)
        def _():
            right_copy(item).wait_recv()

        @pl.when(me < units - 1)
        def _():
            send_right[item] = part[item] + recv_right[item]
            right_copy(item).start()

    def forward_left(item, c, it):
        @pl.when(me < units - 1)
        def _():
            left_copy(item).wait_recv()

        @pl.when(me > 0)
        def _():
            send_left[item] = part[item] + recv_left[item]
            left_copy(item).start()

    far = jnp.maximum(me, units - 1 - me)

    @pl.loop(0, (ITERS - 1) * stride + chunks + units - 1)
    def _(slot):
        at_slot(slot, lambda item, c, it: compute(item, c))
        at_slot(slot - me, forward_right)
        at_slot(slot - (units - 1 - me), forward_left)
        at_slot(slot, settle_nodes)
        at_slot(slot - far, settle_seats)

    for step in range(1, slices):
        stat_copy(lax.rem(mine + step, slices), mine).wait_send()
    for step in range(1, units):
        unit_copy(lax.rem(me + step, units), me).wait_send()

    @pl.loop(0, ITERS * chunks)
    def _(item):
        for side in range(2):
            price_copy(side, item).wait_send()
            in_copy(side, item).wait_send()

        @pl.when(me < units - 1)
        def _():
            right_copy(item).wait_send()

        @pl.when(me > 0)
        def _():
            left_copy(item).wait_send()


def local(
    units, weeks, flow_start, node_start, seat_start, arc_cost, demand, seat_counts, tail_node,
    head_node, cover_row,
):
    scen, arcs = flow_start.shape[2:]
    nodes = node_start.shape[3]
    trips = seat_start.shape[2]
    node_blocks, trip_blocks, arc_blocks = nodes // 128, trips // 128, arcs // 128
    cover_blocks = cover_row.shape[2] // 128
    heads = head_node.reshape(arc_blocks, 128)
    tails = tail_node.reshape(arc_blocks, 128)
    targets = cover_row.reshape(cover_blocks, 128)
    target_block = targets[:, 0] // 128
    order = jnp.arange(cover_blocks, dtype=jnp.int32)
    same = target_block[:, None] == target_block[None, :]
    earlier = order[None, :] < order[:, None]
    previous = jnp.max(jnp.where(same & earlier, order[None, :] + 1, 0), axis=1)
    wanted = jnp.arange(trip_blocks, dtype=jnp.int32)[:, None] == target_block[None, :]
    last = jnp.max(jnp.where(wanted, order[None, :] + 1, 0), axis=1)
    meta = jnp.concatenate([heads[:, 0] // 128, tails[:, 0] // 128, target_block, previous, last])

    chunks = CHUNKS
    rows = scen // chunks
    items = ITERS * chunks
    slices = 2 * weeks
    vmem = pl.BlockSpec(memory_space=pltpu.VMEM)
    smem = pl.BlockSpec(memory_space=pltpu.SMEM)
    dma = pltpu.SemaphoreType.DMA
    flows, prices, seats = pl.pallas_call(
        functools.partial(kernel, units, weeks, chunks),
        out_shape=(
            jax.ShapeDtypeStruct((scen, arcs), F32),
            jax.ShapeDtypeStruct((scen, nodes), F32),
            jax.ShapeDtypeStruct((scen, trips), F32),
        ),
        in_specs=[vmem, vmem, vmem, vmem, vmem, smem, vmem, vmem, vmem, smem],
        out_specs=(vmem, vmem, vmem),
        scratch_shapes=[
            pltpu.VMEM((arc_blocks, 256, 128), BF16),
            pltpu.VMEM((cover_blocks, 128, 128), BF16),
            pltpu.VMEM((chunks * trip_blocks, rows, 128), F32),
            pltpu.VMEM((3 * node_blocks, rows, 128), F32),
            pltpu.VMEM((cover_blocks + 1, rows, 128), F32),
            pltpu.VMEM((items, node_blocks, rows, 128), F32),
            pltpu.VMEM((2, items, node_blocks, rows, 128), F32),
            pltpu.VMEM((items, node_blocks, rows, 128), F32),
            pltpu.VMEM((2, items, node_blocks, rows, 128), F32),
            pltpu.VMEM((2, items, node_blocks, rows, 128), F32),
        ]
        + [pltpu.VMEM((items, trip_blocks, rows, 128), F32)] * 5
        + [
            pltpu.VMEM((scen + 8, 128), F32),
            pltpu.VMEM((slices, scen + 8, 128), F32),
            pltpu.VMEM((8, 128), F32),
            pltpu.VMEM((units, 8, 128), F32),
            pltpu.VMEM((scen, 128), F32),
            pltpu.VMEM((scen, 128), F32),
            dma((slices,)), dma((slices,)), dma((units,)), dma((units,)),
            dma((2, items)), dma((2, items)), dma((2, items)), dma((2, items)),
            dma((items,)), dma((items,)), dma((items,)), dma((items,)),
        ],
        compiler_params=pltpu.CompilerParams(
            collective_id=0, has_side_effects=True, vmem_limit_bytes=48 * 1024 * 1024
        ),
        cost_estimate=pl.CostEstimate(
            flops=12 * scen * arcs * 128, bytes_accessed=8 * scen * arcs, transcendentals=0
        ),
    )(
        flow_start[0, 0], node_start[0, 0], seat_start[0], arc_cost.reshape(arc_blocks, 128),
        demand[0], seat_counts, tails, heads, targets, meta,
    )
    return flows[None, None], prices[None, None], seats[None]


def solution(mesh):
    shape = dict(mesh.shape)
    by_arc = P(("groups", "unit"), ("week", "region"), None, None)
    by_seat = P(("groups", "week", "region"), None, None)
    flat = P(("groups", "unit"), ("week", "region"), None)
    return jax.shard_map(
        functools.partial(local, shape["unit"], shape["week"]),
        mesh=mesh,
        in_specs=(
            by_arc, by_arc, by_seat, flat, by_seat, P(("groups", "unit")), flat, flat, flat,
        ),
        out_specs=(by_arc, by_arc, by_seat),
        check_vma=False,
    )
```

```python
import functools

import jax
import jax.numpy as jnp
from jax import lax
from jax.experimental import pallas as pl
from jax.experimental.pallas import tpu as pltpu
from jax.sharding import PartitionSpec as P

ITERS = 2
WRAP_ARCS = 1024
CROSS_ARCS = 1024
EPS = 1e-06
STEP = 0.5
CHUNKS = 4
UNROLL = 8
BATCH = 8
PIECES = 4
DIMS = (((1,), (1,)), ((), ()))
MESH = pl.DeviceIdType.MESH
F32 = jnp.float32
BF16 = jnp.bfloat16


def split_rows(value):
    high = value.astype(BF16)
    low = (value - high.astype(F32)).astype(BF16)
    return jnp.concatenate([high, low], axis=0)


def pick(block, index):
    return jnp.take_along_axis(block, index, axis=1, mode="promise_in_bounds")


def kernel(
    units, weeks, chunks,
    flow_hbm, node_hbm, seat_hbm, cost_hbm, demand_hbm, count_ref, tail_hbm, head_hbm, cover_hbm,
    meta_ref,
    flow_out, node_out, seat_out,
    node_ref, seat_ref, cost_ref, demand_ref, tail_ref, head_ref, cover_ref, load_sem,
    hot_ends, hot_cover, covers, price_local, spread, chain, own_price, recv_price, own_balance, send_in,
    recv_in, part, send_right, send_left, recv_right, recv_left, stat_mine, stat_slices, cost_mine,
    cost_units, primal, dual,
    stat_send, stat_recv, unit_send, unit_recv, price_send, price_recv, in_send, in_recv,
    right_send, right_recv, left_send, left_recv,
):
    me = lax.axis_index("unit")
    week = lax.axis_index("week")
    region = lax.axis_index("region")
    scen, arcs = flow_out.shape
    nodes = node_ref.shape[1]
    trips = seat_ref.shape[1]
    rows = scen // chunks
    node_blocks = nodes // 128
    trip_blocks = trips // 128
    arc_blocks = arcs // 128
    share = trip_blocks // PIECES
    cover_blocks = cover_ref.shape[0]
    slices = 2 * weeks
    mine = week * 2 + region
    ahead = lax.rem(week + 1, weeks)
    behind = lax.rem(week + weeks - 1, weeks)
    stride = max(chunks, units - 1)
    scale = count_ref[0] / units

    loads = [
        pltpu.make_async_copy(source, target, load_sem.at[n])
        for n, (source, target) in enumerate(
            (
                (demand_hbm, demand_ref), (cost_hbm, cost_ref), (node_hbm, node_ref),
                (head_hbm, head_ref), (tail_hbm, tail_ref), (cover_hbm, cover_ref),
                (seat_hbm, seat_ref), (flow_hbm, flow_out),
            )
        )
    ]
    for load in loads:
        load.start()

    barrier = pltpu.get_barrier_semaphore()
    for step in range(1, units):
        other = lax.rem(me + step, units)
        pl.semaphore_signal(barrier, inc=1, device_id={"unit": other}, device_id_type=MESH)
    for step in range(1, slices):
        other = lax.rem(mine + step, slices)
        pl.semaphore_signal(
            barrier, inc=1, device_id={"week": other // 2, "region": other % 2},
            device_id_type=MESH,
        )

    for load in loads[0:3]:
        load.wait()
    demand_squares = jnp.zeros((scen, 128), F32)
    for block in range(trip_blocks):
        piece = demand_ref[:, block * 128 : block * 128 + 128]
        demand_squares += piece * piece
    cost_squares = jnp.zeros((8, 128), F32)
    for block in range(arc_blocks // 8):
        piece = cost_ref[block * 8 : block * 8 + 8, :]
        cost_squares += piece * piece
    stat_mine[0:scen, :] = demand_squares
    stat_mine[scen : scen + 8, :] = cost_squares
    for c in range(chunks):
        for block in range(node_blocks):
            own_price[c, block] = node_ref[
                c * rows : c * rows + rows, block * 128 : block * 128 + 128
            ]
    pl.semaphore_wait(barrier, units - 1 + slices - 1)

    def stat_copy(other, slot):
        return pltpu.make_async_remote_copy(
            src_ref=stat_mine, dst_ref=stat_slices.at[slot], send_sem=stat_send.at[other],
            recv_sem=stat_recv.at[slot],
            device_id={"week": other // 2, "region": other % 2}, device_id_type=MESH,
        )

    def unit_copy(other, slot):
        return pltpu.make_async_remote_copy(
            src_ref=cost_mine, dst_ref=cost_units.at[slot], send_sem=unit_send.at[other],
            recv_sem=unit_recv.at[slot], device_id={"unit": other}, device_id_type=MESH,
        )

    def price_copy(side, item):
        target = {"week": behind} if side == 0 else {"region": 1 - region}
        return pltpu.make_async_remote_copy(
            src_ref=own_price.at[item], dst_ref=recv_price.at[side, item],
            send_sem=price_send.at[side, item], recv_sem=price_recv.at[side, item],
            device_id=target, device_id_type=MESH,
        )

    def in_copy(side, item):
        target = {"week": ahead} if side == 0 else {"region": 1 - region}
        return pltpu.make_async_remote_copy(
            src_ref=send_in.at[side, item], dst_ref=recv_in.at[side, item],
            send_sem=in_send.at[side, item], recv_sem=in_recv.at[side, item],
            device_id=target, device_id_type=MESH,
        )

    def right_copy(item, q):
        some = pl.ds(q * share, share)
        return pltpu.make_async_remote_copy(
            src_ref=send_right.at[item, some], dst_ref=recv_right.at[item, some],
            send_sem=right_send.at[item, q], recv_sem=right_recv.at[item, q],
            device_id={"unit": lax.rem(me + 1, units)}, device_id_type=MESH,
        )

    def left_copy(item, q):
        some = pl.ds(q * share, share)
        return pltpu.make_async_remote_copy(
            src_ref=send_left.at[item, some], dst_ref=recv_left.at[item, some],
            send_sem=left_send.at[item, q], recv_sem=left_recv.at[item, q],
            device_id={"unit": lax.rem(me + units - 1, units)}, device_id_type=MESH,
        )

    for step in range(1, slices):
        stat_copy(lax.rem(mine + step, slices), mine).start()
    for c in range(chunks):
        price_copy(0, c).start()
        price_copy(1, c).start()

    for load in loads[3:]:
        load.wait()

    sub = lax.broadcasted_iota(jnp.int32, (128, 128), 0)

    def hot(row):
        return jnp.where(jnp.broadcast_to(row, (128, 128)) == sub, 1.0, 0.0).astype(BF16)

    @pl.loop(0, arc_blocks // 8)
    def _(group):
        at = pl.ds(pl.multiple_of(group * 8, 8), 8)
        heads = head_ref[at, :] & 127
        tails = tail_ref[at, :] & 127
        for k in range(8):
            hot_ends[group * 8 + k, 0:128, :] = hot(heads[k : k + 1, :])
            hot_ends[group * 8 + k, 128:256, :] = hot(tails[k : k + 1, :])

    @pl.loop(0, cover_blocks // 8)
    def _(group):
        at = pl.ds(pl.multiple_of(group * 8, 8), 8)
        targets = cover_ref[at, :] & 127
        for k in range(8):
            hot_cover[group * 8 + k] = hot(targets[k : k + 1, :])

    for c in range(chunks):
        for block in range(trip_blocks):
            covers[c * trip_blocks + block] = seat_ref[
                c * rows : c * rows + rows, block * 128 : block * 128 + 128
            ]
    chain[0] = jnp.zeros((rows, 128), F32)

    @pl.when(me == 0)
    def _():
        recv_right[...] = jnp.zeros_like(recv_right)

    @pl.when(me == units - 1)
    def _():
        recv_left[...] = jnp.zeros_like(recv_left)

    for step in range(1, slices):
        stat_copy(mine, lax.rem(mine + step, slices)).wait_recv()
    stat_total = stat_mine[...]
    for step in range(1, slices):
        stat_total += stat_slices[lax.rem(mine + step, slices)]
    cost_mine[...] = stat_total[scen : scen + 8, :]
    for step in range(1, units):
        unit_copy(lax.rem(me + step, units), me).start()
    for step in range(1, units):
        unit_copy(me, lax.rem(me + step, units)).wait_recv()
    cost_total = cost_mine[...]
    for step in range(1, units):
        cost_total += cost_units[lax.rem(me + step, units)]
    cost_sum = jnp.sum(jnp.sum(cost_total, axis=0, keepdims=True), axis=1, keepdims=True)
    demand_sum = jnp.sum(stat_total[0:scen, :], axis=1, keepdims=True)
    ratio = jnp.sqrt(
        (cost_sum / (arcs * units * slices) + EPS) / (demand_sum / (trips * slices) + EPS)
    )
    primal[...] = jnp.broadcast_to(STEP / ratio, (scen, 128))
    dual[...] = jnp.broadcast_to(STEP * ratio, (scen, 128))

    head_at, tail_at = 0, arc_blocks
    cover_at = 2 * arc_blocks
    prev_at = cover_at + cover_blocks
    last_at = prev_at + cover_blocks
    cross = arc_blocks - CROSS_ARCS // 128
    wrap = cross - WRAP_ARCS // 128

    def compute(item, c):
        there = pl.ds(pl.multiple_of(c * rows, 8), rows)
        price_copy(0, item).wait_recv()
        price_copy(1, item).wait_recv()
        price_local[0:node_blocks] = own_price[item]
        price_local[node_blocks : 2 * node_blocks] = recv_price[0, item]
        price_local[2 * node_blocks : 3 * node_blocks] = recv_price[1, item]
        step_size = primal[there, :]

        def section(first, end, side, with_cover, start):
            def body(group, carry):
                own, away = list(carry[0]), list(carry[1])
                base = first + group * UNROLL
                at = pl.ds(pl.multiple_of(base, 8), UNROLL)
                heads = head_ref[at, :] & 127
                tails = tail_ref[at, :] & 127
                costs = cost_ref[at, :]
                if with_cover:
                    targets = cover_ref[at, :] & 127
                for first_k in range(0, UNROLL, BATCH):
                    batch = range(first_k, first_k + BATCH)
                    head_block = [meta_ref[head_at + base + k] for k in batch]
                    tail_block = [meta_ref[tail_at + base + k] for k in batch]
                    column = [pl.ds(pl.multiple_of((base + k) * 128, 128), 128) for k in batch]
                    head_price = [price_local[side * node_blocks + m] for m in head_block]
                    tail_price = [price_local[m] for m in tail_block]
                    now = [flow_out[there, at] for at in column]
                    if with_cover:
                        cover_price = [
                            covers[c * trip_blocks + meta_ref[cover_at + base + k]] for k in batch
                        ]
                    updated, halves = [], []
                    for n, k in enumerate(batch):
                        wide = lambda row: jnp.broadcast_to(row[k : k + 1, :], (rows, 128))
                        gradient = wide(costs)
                        if with_cover:
                            gradient = gradient - scale * pick(cover_price[n], wide(targets))
                        gradient = gradient - (
                            pick(head_price[n], wide(heads)) - pick(tail_price[n], wide(tails))
                        )
                        updated.append(jnp.maximum(now[n] - step_size * gradient, 0.0))
                        halves.append(split_rows(2.0 * updated[n] - now[n]))
                    tables = [hot_ends[base + k] for k in batch]
                    ends = [
                        lax.dot_general(
                            halves[n], tables[n], DIMS, preferred_element_type=F32
                        )
                        for n in range(BATCH)
                    ]
                    if with_cover:
                        filled = [
                            lax.dot_general(
                                halves[n], hot_cover[base + k], DIMS, preferred_element_type=F32
                            )
                            for n, k in enumerate(batch)
                        ]
                    for n in range(BATCH):
                        flow_out[there, column[n]] = updated[n]
                    for n in range(BATCH):
                        total = ends[n][0:rows] + ends[n][rows : 2 * rows]
                        into, outof = total[:, 0:128], total[:, 128:256]
                        for m in range(node_blocks):
                            landed = jnp.where(head_block[n] == m, into, 0.0)
                            left = jnp.where(tail_block[n] == m, outof, 0.0)
                            if side == 0:
                                own[m] = own[m] + (landed - left)
                            else:
                                own[m] = own[m] - left
                                away[m] = away[m] + landed
                    if with_cover:
                        for n, k in enumerate(batch):
                            spread[base + k] = scale * (
                                filled[n][0:rows] + filled[n][rows : 2 * rows]
                            )
                return tuple(own), tuple(away)

            return lax.fori_loop(0, (end - first) // UNROLL, body, start)

        zeros = tuple(jnp.zeros((rows, 128), F32) for _ in range(node_blocks))
        own, _ = section(0, cover_blocks, 0, True, (zeros, ()))
        own, _ = section(cover_blocks, wrap, 0, False, (own, ()))
        own, away_next = section(wrap, cross, 1, False, (own, zeros))
        own, away_other = section(cross, arc_blocks, 2, False, (own, zeros))
        for m in range(node_blocks):
            own_balance[item, m] = own[m]
            send_in[0, item, m] = away_next[m]
            send_in[1, item, m] = away_other[m]
        in_copy(0, item).start()
        in_copy(1, item).start()
        for b in range(cover_blocks):
            chain[b + 1] = spread[b] + chain[meta_ref[prev_at + b]]
        for m in range(trip_blocks):
            part[item, m] = chain[meta_ref[last_at + m]]

    def settle_nodes(item, c, it):
        there = pl.ds(pl.multiple_of(c * rows, 8), rows)
        in_copy(0, item).wait_recv()
        in_copy(1, item).wait_recv()
        step_size = dual[there, :]

        def priced(m):
            balance = own_balance[item, m] + recv_in[0, item, m] + recv_in[1, item, m]
            return own_price[item, m] - step_size * balance

        @pl.when(it < ITERS - 1)
        def _():
            for m in range(node_blocks):
                own_price[item + chunks, m] = priced(m)
            price_copy(0, item + chunks).start()
            price_copy(1, item + chunks).start()

        @pl.when(it == ITERS - 1)
        def _():
            for m in range(node_blocks):
                node_out[there, m * 128 : m * 128 + 128] = priced(m)

    def settle_seats(item, c, it):
        there = pl.ds(pl.multiple_of(c * rows, 8), rows)
        step_size = dual[there, :]

        def covered(m):
            total = recv_right[item, m] + part[item, m] + recv_left[item, m]
            wanted = demand_ref[there, m * 128 : m * 128 + 128]
            return jnp.maximum(
                covers[c * trip_blocks + m] + step_size * (wanted - total), 0.0
            )

        @pl.when(it < ITERS - 1)
        def _():
            for m in range(trip_blocks):
                covers[c * trip_blocks + m] = covered(m)

        @pl.when(it == ITERS - 1)
        def _():
            for m in range(trip_blocks):
                seat_out[there, m * 128 : m * 128 + 128] = covered(m)

    def at_slot(slot, action):
        it = slot // stride
        c = slot % stride

        @pl.when((slot >= 0) & (c < chunks) & (it < ITERS))
        def _():
            action(it * chunks + c, c, it)

    def forward_right(q, item, c, it):
        some = pl.ds(q * share, share)

        @pl.when(me > 0)
        def _():
            right_copy(item, q).wait_recv()

        @pl.when(me < units - 1)
        def _():
            send_right[item, some] = part[item, some] + recv_right[item, some]
            right_copy(item, q).start()

    def forward_left(q, item, c, it):
        some = pl.ds(q * share, share)

        @pl.when(me < units - 1)
        def _():
            left_copy(item, q).wait_recv()

        @pl.when(me > 0)
        def _():
            send_left[item, some] = part[item, some] + recv_left[item, some]
            left_copy(item, q).start()

    far = jnp.maximum(me, units - 1 - me)

    @pl.loop(0, (ITERS - 1) * stride + chunks + units - 1)
    def _(slot):
        at_slot(slot, lambda item, c, it: compute(item, c))
        at_slot(slot - 1, settle_nodes)
        for q in range(PIECES):
            at_slot(slot - me, functools.partial(forward_right, q))
            at_slot(slot - (units - 1 - me), functools.partial(forward_left, q))
        at_slot(slot - far, settle_seats)

    for step in range(1, slices):
        stat_copy(lax.rem(mine + step, slices), mine).wait_send()
    for step in range(1, units):
        unit_copy(lax.rem(me + step, units), me).wait_send()

    @pl.loop(0, ITERS * chunks)
    def _(item):
        for side in range(2):
            price_copy(side, item).wait_send()
            in_copy(side, item).wait_send()

        @pl.when(me < units - 1)
        def _():
            for q in range(PIECES):
                right_copy(item, q).wait_send()

        @pl.when(me > 0)
        def _():
            for q in range(PIECES):
                left_copy(item, q).wait_send()


def local(
    units, weeks, flow_start, node_start, seat_start, arc_cost, demand, seat_counts, tail_node,
    head_node, cover_row,
):
    scen, arcs = flow_start.shape[2:]
    nodes = node_start.shape[3]
    trips = seat_start.shape[2]
    node_blocks, trip_blocks, arc_blocks = nodes // 128, trips // 128, arcs // 128
    cover_blocks = cover_row.shape[2] // 128
    heads = head_node.reshape(arc_blocks, 128)
    tails = tail_node.reshape(arc_blocks, 128)
    targets = cover_row.reshape(cover_blocks, 128)
    target_block = targets[:, 0] // 128
    order = jnp.arange(cover_blocks, dtype=jnp.int32)
    same = target_block[:, None] == target_block[None, :]
    earlier = order[None, :] < order[:, None]
    previous = jnp.max(jnp.where(same & earlier, order[None, :] + 1, 0), axis=1)
    wanted = jnp.arange(trip_blocks, dtype=jnp.int32)[:, None] == target_block[None, :]
    last = jnp.max(jnp.where(wanted, order[None, :] + 1, 0), axis=1)
    meta = jnp.concatenate([heads[:, 0] // 128, tails[:, 0] // 128, target_block, previous, last])

    chunks = CHUNKS
    rows = scen // chunks
    items = ITERS * chunks
    slices = 2 * weeks
    vmem = pl.BlockSpec(memory_space=pltpu.VMEM)
    smem = pl.BlockSpec(memory_space=pltpu.SMEM)
    hbm = pl.BlockSpec(memory_space=pltpu.HBM)
    dma = pltpu.SemaphoreType.DMA
    flows, prices, seats = pl.pallas_call(
        functools.partial(kernel, units, weeks, chunks),
        out_shape=(
            jax.ShapeDtypeStruct((scen, arcs), F32),
            jax.ShapeDtypeStruct((scen, nodes), F32),
            jax.ShapeDtypeStruct((scen, trips), F32),
        ),
        in_specs=[hbm, hbm, hbm, hbm, hbm, smem, hbm, hbm, hbm, smem],
        out_specs=(vmem, vmem, vmem),
        scratch_shapes=[
            pltpu.VMEM((scen, nodes), F32),
            pltpu.VMEM((scen, trips), F32),
            pltpu.VMEM((arc_blocks, 128), F32),
            pltpu.VMEM((scen, trips), F32),
            pltpu.VMEM((arc_blocks, 128), jnp.int32),
            pltpu.VMEM((arc_blocks, 128), jnp.int32),
            pltpu.VMEM((cover_blocks, 128), jnp.int32),
            dma((8,)),
            pltpu.VMEM((arc_blocks, 256, 128), BF16),
            pltpu.VMEM((cover_blocks, 128, 128), BF16),
            pltpu.VMEM((chunks * trip_blocks, rows, 128), F32),
            pltpu.VMEM((3 * node_blocks, rows, 128), F32),
            pltpu.VMEM((cover_blocks, rows, 128), F32),
            pltpu.VMEM((cover_blocks + 1, rows, 128), F32),
            pltpu.VMEM((items, node_blocks, rows, 128), F32),
            pltpu.VMEM((2, items, node_blocks, rows, 128), F32),
            pltpu.VMEM((items, node_blocks, rows, 128), F32),
            pltpu.VMEM((2, items, node_blocks, rows, 128), F32),
            pltpu.VMEM((2, items, node_blocks, rows, 128), F32),
        ]
        + [pltpu.VMEM((items, trip_blocks, rows, 128), F32)] * 5
        + [
            pltpu.VMEM((scen + 8, 128), F32),
            pltpu.VMEM((slices, scen + 8, 128), F32),
            pltpu.VMEM((8, 128), F32),
            pltpu.VMEM((units, 8, 128), F32),
            pltpu.VMEM((scen, 128), F32),
            pltpu.VMEM((scen, 128), F32),
            dma((slices,)), dma((slices,)), dma((units,)), dma((units,)),
            dma((2, items)), dma((2, items)), dma((2, items)), dma((2, items)),
            dma((items, PIECES)), dma((items, PIECES)), dma((items, PIECES)), dma((items, PIECES)),
        ],
        compiler_params=pltpu.CompilerParams(
            collective_id=0, has_side_effects=True, vmem_limit_bytes=62 * 1024 * 1024
        ),
        cost_estimate=pl.CostEstimate(
            flops=12 * scen * arcs * 128, bytes_accessed=8 * scen * arcs, transcendentals=0
        ),
    )(
        flow_start[0, 0], node_start[0, 0], seat_start[0], arc_cost.reshape(arc_blocks, 128),
        demand[0], seat_counts, tails, heads, targets, meta,
    )
    return flows[None, None], prices[None, None], seats[None]


def solution(mesh):
    shape = dict(mesh.shape)
    by_arc = P(("groups", "unit"), ("week", "region"), None, None)
    by_seat = P(("groups", "week", "region"), None, None)
    flat = P(("groups", "unit"), ("week", "region"), None)
    return jax.shard_map(
        functools.partial(local, shape["unit"], shape["week"]),
        mesh=mesh,
        in_specs=(
            by_arc, by_arc, by_seat, flat, by_seat, P(("groups", "unit")), flat, flat, flat,
        ),
        out_specs=(by_arc, by_arc, by_seat),
        check_vma=False,
    )
```
